32 devices in a mesh: chan: 8 (over z, y), win: 4 (over x, core).
Axes of the slice: x: 2, y: 2, z: 4, core: 2. Of those that a mesh axis runs over, the one named last changes fastest.
Arguments:
- samples: int32 [1536, 8, 6144], P('chan', 'win'), may hold values from -2048 to 2046
- exponents: int32 [1536, 8, 24], P('chan', 'win'), may hold values from 0 to 4
- alive: int32 [1536], P('chan'), may hold values 0 or 1
- offsets: int32 [32], P('chan'), may hold values from 0 to 191
Outputs:
- stacks: float32 [32, 384, 2048], P('chan', 'win')
The draws below stay inside these ranges and needn't reach their ends.
All inputs are finite; a program needn't handle non-finite values. No bound on the sum of `alive` on one device may be relied on, other than what follows from the above.
Results may differ from the reference program's by a relative error of at most 0.0032.
Values may be sent and summed in bfloat16 or wider, within the bound.
A program may use at most 256 MiB of HBM per device.

```python
import math
import jax
import jax.numpy as jnp
from jax import lax

CH_DEV = 192
SRC_DEV = 4
SEG = 1024
BAND = 192
TW = 6144
NBLK = 24
CHANNELS = 1536
NSRC = 32
WINDOWS = 8


def draw_samples(key, part):
    wave_key = jax.random.fold_in(key, 11)
    noise_key = jax.random.fold_in(key, 12)
    source_wave = jax.random.randint(wave_key, (WINDOWS, TW + CHANNELS), -1024, 1024, dtype=jnp.int32)
    positions = jnp.arange(CHANNELS, dtype=jnp.int32)[:, None] + jnp.arange(TW, dtype=jnp.int32)[None, :]
    moved = jnp.take(source_wave, positions, axis=1)
    noise_part = jax.random.randint(noise_key, (CHANNELS, WINDOWS, TW), -1024, 1024, dtype=jnp.int32)
    return jnp.transpose(moved, (1, 0, 2)) + noise_part


def plant(entries, key, least, top_value):
    spot = [jax.random.randint(jax.random.fold_in(key, axis), (), 0, length) for axis, length in enumerate(entries.shape)]
    main_axis = entries.shape.index(max(entries.shape))
    beside = spot[:main_axis] + [(spot[main_axis] + 1) % entries.shape[main_axis]] + spot[main_axis + 1:]
    return entries.at[tuple(spot)].set(least).at[tuple(beside)].set(top_value)


def setup_inputs(seed: int = 0) -> dict:
    keys = jax.random.split(jax.random.key(seed), 5)
    return {
        "samples": draw_samples(jax.random.fold_in(keys[4], 71), 0),
        "exponents": plant(jax.random.randint(keys[1], (CHANNELS, WINDOWS, NBLK), 0, 5), jax.random.fold_in(keys[1], 1), 0, 4).astype(jnp.int32),
        "alive": plant((jax.random.randint(keys[2], (CHANNELS,), 0, 10) < 9).astype(jnp.int32), jax.random.fold_in(keys[2], 1), 0, 1),
        "offsets": plant(jax.random.randint(keys[3], (NSRC,), 0, CH_DEV), jax.random.fold_in(keys[3], 1), 0, CH_DEV - 1).astype(jnp.int32),
    }


def block_scale(exponents):
    levels = jnp.arange(5, dtype=jnp.int32)
    powers = jnp.exp2(levels.astype(jnp.float32))
    return lax.optimization_barrier(jnp.sum(jnp.where(exponents[..., None] == levels, powers, 0.0), axis=-1))

def normalize(samples, exponents, alive):
    channels, windows, length = samples.shape
    block_count = exponents.shape[2]
    amplitude = samples.astype(jnp.float32).reshape(channels, windows, block_count, length // block_count)
    amplitude = amplitude * block_scale(exponents)[..., None]
    energy = lax.optimization_barrier(jnp.mean(amplitude * amplitude, axis=(2, 3), keepdims=True))
    factor = alive.astype(jnp.float32)[:, None, None, None] * lax.rsqrt(energy + 1e-06)
    return (amplitude * factor).reshape(channels, windows, length).astype(jnp.bfloat16)

def forward_basis(seg_len):
    full_len = 2 * seg_len
    sample_index = jnp.arange(seg_len, dtype=jnp.int32)
    phases = sample_index[:, None] * sample_index[None, :] % full_len
    angles = phases.astype(jnp.float32) * (2.0 * math.pi / full_len)
    return jnp.concatenate([jnp.cos(angles), -jnp.sin(angles)], axis=1).astype(jnp.bfloat16)

def transform(normed, seg_len):
    channels, windows, length = normed.shape
    seg_count = length // seg_len
    segments = normed.reshape(channels * windows * seg_count, seg_len)
    spectra = jnp.dot(segments, forward_basis(seg_len), preferred_element_type=jnp.float32).astype(jnp.bfloat16)
    return spectra.reshape(channels, windows * seg_count, 2 * seg_len)

def inverse_table(seg_len, windows, seg_count):
    full_len = 2 * seg_len
    bin_index = jnp.arange(seg_len, dtype=jnp.int32)
    lag_index = jnp.arange(full_len, dtype=jnp.int32) - full_len // 2
    phases = bin_index[:, None] * lag_index[None, :] % full_len
    angles = phases.astype(jnp.float32) * (2.0 * math.pi / full_len)
    weight = jnp.where(bin_index == 0, 1.0, 2.0).astype(jnp.float32) / float(full_len * windows * seg_count * seg_len)
    return jnp.concatenate([weight[:, None] * jnp.cos(angles), -weight[:, None] * jnp.sin(angles)], axis=0)

def cross_spectra(source, band_rows):
    bin_count = source.shape[1] // 2
    src_re = source[:, :bin_count]
    src_im = source[:, bin_count:]
    band_re = band_rows[..., :bin_count]
    band_im = band_rows[..., bin_count:]
    real_part = lax.optimization_barrier(jnp.sum(src_re * band_re + src_im * band_im, axis=1))
    imag_part = lax.optimization_barrier(jnp.sum(src_re * band_im - src_im * band_re, axis=1))
    return jnp.concatenate([real_part, imag_part], axis=-1)

def reference(samples, exponents, alive, offsets):
    channels, windows, length = samples.shape
    seg_count = length // SEG
    normed = normalize(samples, exponents, alive)
    blocks = normed.reshape(channels // CH_DEV, CH_DEV, windows, length)

    def block_spectra(block):
        return transform(block, SEG)
    spectra = lax.map(block_spectra, blocks).reshape(channels, windows * seg_count, 2 * SEG)
    padded = jnp.pad(spectra, ((BAND, BAND), (0, 0), (0, 0)))
    src_chan = jnp.arange(NSRC, dtype=jnp.int32) // SRC_DEV * CH_DEV + offsets.astype(jnp.int32)
    lag_table = inverse_table(SEG, windows, seg_count)

    def one_source(first_row):
        source = lax.dynamic_index_in_dim(padded, first_row + BAND, 0, keepdims=False).astype(jnp.float32)
        band_rows = lax.dynamic_slice_in_dim(padded, first_row, 2 * BAND, 0).astype(jnp.float32)
        terms = cross_spectra(source, band_rows)
        return jnp.dot(terms, lag_table, precision=lax.Precision.HIGHEST, preferred_element_type=jnp.float32)
    return lax.map(one_source, src_chan)
```

```python
import functools

import jax
import jax.numpy as jnp
import ml_dtypes
import numpy as np
from jax import lax
from jax.experimental import pallas as pl
from jax.experimental.pallas import tpu as pltpu
from jax.sharding import PartitionSpec as P

SEG = 1024
SCALE_LEN = 256
GROUP = 16
F32, BF16 = jnp.float32, jnp.bfloat16


def bin_order():
    bins = np.arange(SEG).reshape(-1, 1, GROUP)
    return np.concatenate([bins, bins + SEG], axis=1).reshape(-1)


@functools.lru_cache(None)
def forward_basis():
    i = np.arange(SEG)
    angles = (i[:, None] * i[None, :] % (2 * SEG)) * (2.0 * np.pi / (2 * SEG))
    basis = np.concatenate([np.cos(angles), -np.sin(angles)], axis=1)
    return basis.astype(np.float32).astype(ml_dtypes.bfloat16)


@functools.lru_cache(None)
def lag_tables(windows, seg_count):
    full = 2 * SEG
    k = np.arange(SEG)
    lag = np.arange(full) - SEG
    angles = (k[:, None] * lag[None, :] % full) * (2.0 * np.pi / full)
    weight = np.where(k == 0, 1.0, 2.0)[:, None] / float(full * windows * seg_count * SEG)
    table = np.concatenate([weight * np.cos(angles), -weight * np.sin(angles)], axis=0)
    table = table[bin_order()].astype(np.float32)
    high = table.astype(ml_dtypes.bfloat16)
    low = (table - high.astype(np.float32)).astype(ml_dtypes.bfloat16)
    return high, low


def norm_kernel(samples, exponents, alive, out, raw, sems):
    windows, channels, length = raw.shape
    copies = [
        pltpu.make_async_copy(samples.at[:, w, :], raw.at[w], sems.at[w]) for w in range(windows)
    ]
    for copy in copies:
        copy.start()
    for w in range(windows):
        copies[w].wait()
        scale = jnp.left_shift(1, exponents[w]).astype(F32)
        total = jnp.zeros((channels, SCALE_LEN), F32)
        for b in range(length // SCALE_LEN):
            x = raw[w, :, b * SCALE_LEN : (b + 1) * SCALE_LEN].astype(F32) * scale[:, b : b + 1]
            total = total + x * x
        energy = jnp.sum(total, axis=1, keepdims=True) / length
        factor = alive[...] * lax.rsqrt(energy + 1e-06)
        for b in range(length // SCALE_LEN):
            x = raw[w, :, b * SCALE_LEN : (b + 1) * SCALE_LEN].astype(F32) * scale[:, b : b + 1]
            n, part = divmod(b * SCALE_LEN, SEG)
            out[w * (length // SEG) + n, part : part + SCALE_LEN, :] = (x * factor).T.astype(BF16)


def normalize_blocks(samples, exponents, alive):
    channels, windows, length = samples.shape
    return pl.pallas_call(
        norm_kernel,
        out_shape=jax.ShapeDtypeStruct((windows * length // SEG, SEG, channels), BF16),
        in_specs=[
            pl.BlockSpec(memory_space=pl.ANY),
            pl.BlockSpec(memory_space=pltpu.VMEM),
            pl.BlockSpec(memory_space=pltpu.VMEM),
        ],
        out_specs=pl.BlockSpec(memory_space=pltpu.VMEM),
        scratch_shapes=[
            pltpu.VMEM((windows, channels, length), jnp.int32),
            pltpu.SemaphoreType.DMA((windows,)),
        ],
        compiler_params=pltpu.CompilerParams(vmem_limit_bytes=48 * 2**20),
    )(samples, jnp.swapaxes(exponents, 0, 1), alive.astype(F32)[:, None])


def cross_kernel(offsets, basis, blocks, rows, out, spec, weights, cross):
    seg_count, _, channels = blocks.shape
    groups, terms, depth = rows.shape
    sources = terms // 2
    for n in range(seg_count):
        part = jnp.dot(basis[...], blocks[n], preferred_element_type=F32).astype(BF16)
        for q in range(groups):
            spec[q, n * 2 * GROUP : (n + 1) * 2 * GROUP, :] = part[q * 2 * GROUP : (q + 1) * 2 * GROUP]
    lane_bin = lax.broadcasted_iota(jnp.int32, (GROUP, depth), 1) % GROUP
    same = lane_bin == lax.broadcasted_iota(jnp.int32, (GROUP, depth), 0)
    for q in range(groups):
        for s in range(terms):
            row = jnp.broadcast_to(rows[q, s : s + 1, :], (GROUP, depth))
            weights[q % 2, s * GROUP : (s + 1) * GROUP, :] = jnp.where(same, row, 0.0).astype(BF16)
        product = jnp.dot(weights[q % 2], spec[q], preferred_element_type=F32).astype(BF16)
        for s in range(sources):
            cross[s, q * 2 * GROUP : (q + 1) * 2 * GROUP, :] = product[s * 2 * GROUP : (s + 1) * 2 * GROUP]
    target = lax.broadcasted_iota(jnp.int32, (channels, channels), 0)
    origin = lax.broadcasted_iota(jnp.int32, (channels, channels), 1)
    half = channels // 2
    for s in range(sources):
        at = target + offsets[s]
        at = jnp.where(at >= channels, at - channels, at)
        turn = jnp.where(at == origin, 1.0, 0.0).astype(BF16)
        turned = lax.dot_general(
            turn, cross[s], (((1,), (1,)), ((), ())), preferred_element_type=F32
        ).astype(BF16)
        out[0, s] = turned[:half]
        out[1, s] = turned[half:]


def cross_terms(offsets, blocks, rows, first, count):
    seg_count, _, channels = blocks.shape
    _, terms, depth = rows.shape
    step = 8
    width = step * 2 * GROUP
    basis = jnp.asarray(forward_basis().T[bin_order()][first * 2 * GROUP : (first + count) * 2 * GROUP])
    return pl.pallas_call(
        cross_kernel,
        grid_spec=pltpu.PrefetchScalarGridSpec(
            num_scalar_prefetch=1,
            grid=(count // step,),
            in_specs=[
                pl.BlockSpec((width, SEG), lambda i, o: (i, 0)),
                pl.BlockSpec((seg_count, SEG, channels), lambda i, o: (0, 0, 0)),
                pl.BlockSpec((step, terms, depth), lambda i, o: (i + first // step, 0, 0)),
            ],
            out_specs=pl.BlockSpec((2, terms // 2, channels // 2, width), lambda i, o: (0, 0, 0, i)),
            scratch_shapes=[
                pltpu.VMEM((step, depth, channels), BF16),
                pltpu.VMEM((2, terms * GROUP, depth), BF16),
                pltpu.VMEM((terms // 2, width, channels), BF16),
            ],
        ),
        out_shape=jax.ShapeDtypeStruct((2, terms // 2, channels // 2, count * 2 * GROUP), BF16),
        compiler_params=pltpu.CompilerParams(vmem_limit_bytes=48 * 2**20),
    )(offsets, basis, blocks, rows)


def lag_kernel(kept, came, high, low, out):
    total = kept[...].astype(F32) + came[...].astype(F32)
    top = total.astype(BF16)
    rest = (total - top.astype(F32)).astype(BF16)
    result = jnp.dot(top, low[...], preferred_element_type=F32)
    result = result + jnp.dot(rest, high[...], preferred_element_type=F32)
    out[...] = result + jnp.dot(top, high[...], preferred_element_type=F32)


def lag_product(kept, came, high, low):
    rows, depth = kept.shape
    width = 512
    return pl.pallas_call(
        lag_kernel,
        grid=(2 * SEG // width,),
        in_specs=[
            pl.BlockSpec((rows, depth), lambda i: (0, 0)),
            pl.BlockSpec((rows, depth), lambda i: (0, 0)),
            pl.BlockSpec((depth, width), lambda i: (0, i)),
            pl.BlockSpec((depth, width), lambda i: (0, i)),
        ],
        out_specs=pl.BlockSpec((rows, width), lambda i: (0, i)),
        out_shape=jax.ShapeDtypeStruct((rows, 2 * SEG), F32),
        compiler_params=pltpu.CompilerParams(vmem_limit_bytes=48 * 2**20),
    )(kept, came, high, low)


def passed_along(block, axis, distance):
    devices = range(lax.axis_size(axis))
    route = [(i - distance, i) for i in devices if i - distance in devices]
    return lax.ppermute(block, axis, route)


def swapped(block, bit):
    return lax.ppermute(block, "win", [(i, i ^ bit) for i in range(lax.axis_size("win"))])


def source_rows(samples, exponents, alive, offsets):
    picked = [
        [lax.dynamic_slice_in_dim(a, offsets[j], 1, 0) for j in range(offsets.shape[0])]
        for a in (samples, exponents, alive)
    ]
    samples, exponents, alive = (jnp.concatenate(p, axis=0) for p in picked)
    count, windows, length = samples.shape
    scale = jnp.left_shift(1, exponents).astype(F32)
    amplitude = samples.astype(F32).reshape(count, windows, -1, SCALE_LEN) * scale[..., None]
    energy = jnp.mean(amplitude * amplitude, axis=(2, 3), keepdims=True)
    factor = alive.astype(F32)[:, None, None, None] * lax.rsqrt(energy + 1e-06)
    normed = (amplitude * factor).astype(BF16).reshape(count, windows * length)
    tail = jnp.broadcast_to(offsets.astype(BF16)[:, None], (count, 128))
    return jnp.concatenate([normed, tail], axis=1)


def source_terms(sources):
    count, length = sources.shape
    seg_count = length // SEG
    spectra = jnp.dot(
        sources.reshape(count * seg_count, SEG), jnp.asarray(forward_basis()), preferred_element_type=F32
    ).astype(BF16)
    spectra = spectra.reshape(count, seg_count, 2, SEG // GROUP, GROUP)
    real, imag = spectra[:, :, 0], spectra[:, :, 1]
    pair = jnp.stack([jnp.stack([real, imag], 2), jnp.stack([-imag, real], 2)], 1)
    rows = jnp.transpose(pair, (4, 0, 1, 2, 3, 5))
    return rows.reshape(SEG // GROUP, count * 2, seg_count * 2 * GROUP).astype(F32)


CHUNKS = 1


def shards(samples, exponents, alive, offsets):
    channels, windows, length = samples.shape
    per_device = offsets.shape[0]
    win = lax.axis_index("win")
    core, side = win % 2, win // 2
    own = source_rows(samples, exponents, alive, offsets)
    sources = jnp.concatenate(
        [passed_along(own, "chan", 1), own, passed_along(own, "chan", -1)], axis=0
    )
    places = sources[:, windows * length].astype(jnp.int32)
    rows = source_terms(sources[:, : windows * length])
    blocks = normalize_blocks(samples, exponents, alive)
    half = channels // 2
    turned = (core * half + jnp.arange(half, dtype=jnp.int32))[None, :, None]
    low_part = turned < (channels - offsets)[:, None, None]
    kept, came = [], []
    groups = SEG // GROUP
    count = groups // CHUNKS
    for c in range(CHUNKS):
        terms = cross_terms(places, blocks, rows, c * count, count)
        mine = lax.dynamic_index_in_dim(terms, core, 0, keepdims=False)
        other = swapped(lax.dynamic_index_in_dim(terms, 1 - core, 0, keepdims=False), 1)
        pair = (mine.astype(F32) + other.astype(F32)).astype(BF16)
        below = passed_along(pair[2 * per_device :], "chan", 1)
        above = passed_along(pair[:per_device], "chan", -1)
        here = pair[per_device : 2 * per_device]
        first = jnp.where(low_part, below, here)
        second = jnp.where(low_part, here, above)
        kept.append(jnp.where(side == 0, first, second))
        came.append(swapped(jnp.where(side == 0, second, first), 2))
    kept = jnp.concatenate(kept, axis=-1).reshape(per_device * half, 2 * SEG)
    came = jnp.concatenate(came, axis=-1).reshape(per_device * half, 2 * SEG)
    high, low = lag_tables(windows * lax.axis_size("win"), length // SEG)
    result = lag_product(kept, came, jnp.asarray(high), jnp.asarray(low))
    return result.reshape(per_device, half, 2 * SEG)


def solution(mesh):
    placed = (P("chan", "win", None), P("chan", "win", None), P("chan"), P("chan"))
    return jax.shard_map(
        shards, mesh=mesh, in_specs=placed, out_specs=P("chan", "win", None), check_vma=False
    )
```

```python
import functools

import jax
import jax.numpy as jnp
import ml_dtypes
import numpy as np
from jax import lax
from jax.experimental import pallas as pl
from jax.experimental.pallas import tpu as pltpu
from jax.sharding import PartitionSpec as P

SEG = 1024
SCALE_LEN = 256
GROUP = 16
F32, BF16 = jnp.float32, jnp.bfloat16


def bin_order():
    bins = np.arange(SEG).reshape(-1, 1, GROUP)
    return np.concatenate([bins, bins + SEG], axis=1).reshape(-1)


@functools.lru_cache(None)
def forward_basis():
    i = np.arange(SEG)
    angles = (i[:, None] * i[None, :] % (2 * SEG)) * (2.0 * np.pi / (2 * SEG))
    basis = np.concatenate([np.cos(angles), -np.sin(angles)], axis=1)
    return basis.astype(np.float32).astype(ml_dtypes.bfloat16)


@functools.lru_cache(None)
def lag_tables(windows, seg_count):
    full = 2 * SEG
    k = np.arange(SEG)
    lag = np.arange(full) - SEG
    angles = (k[:, None] * lag[None, :] % full) * (2.0 * np.pi / full)
    weight = np.where(k == 0, 1.0, 2.0)[:, None] / float(full * windows * seg_count * SEG)
    table = np.concatenate([weight * np.cos(angles), -weight * np.sin(angles)], axis=0)
    table = table[bin_order()].astype(np.float32)
    high = table.astype(ml_dtypes.bfloat16)
    low = (table - high.astype(np.float32)).astype(ml_dtypes.bfloat16)
    return high, low


def norm_kernel(samples, exponents, alive, out, raw, sems):
    windows, channels, length = raw.shape
    copies = [
        pltpu.make_async_copy(samples.at[:, w, :], raw.at[w], sems.at[w]) for w in range(windows)
    ]
    for copy in copies:
        copy.start()
    for w in range(windows):
        copies[w].wait()
        scale = jnp.left_shift(1, exponents[w]).astype(F32)
        total = jnp.zeros((channels, SCALE_LEN), F32)
        for b in range(length // SCALE_LEN):
            x = raw[w, :, b * SCALE_LEN : (b + 1) * SCALE_LEN].astype(F32) * scale[:, b : b + 1]
            total = total + x * x
        energy = jnp.sum(total, axis=1, keepdims=True) / length
        factor = alive[...] * lax.rsqrt(energy + 1e-06)
        for b in range(length // SCALE_LEN):
            x = raw[w, :, b * SCALE_LEN : (b + 1) * SCALE_LEN].astype(F32) * scale[:, b : b + 1]
            n, part = divmod(b * SCALE_LEN, SEG)
            out[w * (length // SEG) + n, part : part + SCALE_LEN, :] = (x * factor).T.astype(BF16)


def normalize_blocks(samples, exponents, alive):
    channels, windows, length = samples.shape
    return pl.pallas_call(
        norm_kernel,
        out_shape=jax.ShapeDtypeStruct((windows * length // SEG, SEG, channels), BF16),
        in_specs=[
            pl.BlockSpec(memory_space=pl.ANY),
            pl.BlockSpec(memory_space=pltpu.VMEM),
            pl.BlockSpec(memory_space=pltpu.VMEM),
        ],
        out_specs=pl.BlockSpec(memory_space=pltpu.VMEM),
        scratch_shapes=[
            pltpu.VMEM((windows, channels, length), jnp.int32),
            pltpu.SemaphoreType.DMA((windows,)),
        ],
        compiler_params=pltpu.CompilerParams(vmem_limit_bytes=48 * 2**20),
    )(samples, jnp.swapaxes(exponents, 0, 1), alive.astype(F32)[:, None])


def cross_kernel(offsets, basis, factors, blocks, sources, mine, other, spec, terms, weights, cross):
    seg_count, _, channels = blocks.shape
    groups, depth, _ = spec.shape
    count = mine.shape[0]
    padded = sources.shape[0] // seg_count
    width = groups * 2 * GROUP
    for n in range(seg_count):
        part = jnp.dot(basis[...], blocks[n], preferred_element_type=F32).astype(BF16)
        for q in range(groups):
            spec[q, n * 2 * GROUP : (n + 1) * 2 * GROUP, :] = part[q * 2 * GROUP : (q + 1) * 2 * GROUP]
    terms[...] = (
        jnp.dot(sources[...], factors[0], preferred_element_type=F32).astype(BF16).astype(F32)
    )
    lane_bin = lax.broadcasted_iota(jnp.int32, (GROUP, depth), 1) % GROUP
    same = lane_bin == lax.broadcasted_iota(jnp.int32, (GROUP, depth), 0)
    for q in range(groups):
        for c in range(2):
            at = c * width + q * 2 * GROUP
            rows = jnp.concatenate(
                [terms[n * padded : (n + 1) * padded, at : at + 2 * GROUP] for n in range(seg_count)], axis=1
            )
            for s in range(count):
                row = jnp.broadcast_to(rows[s : s + 1, :], (GROUP, depth))
                start = (2 * s + c) * GROUP
                weights[q % 2, start : start + GROUP, :] = jnp.where(same, row, 0.0).astype(BF16)
        product = jnp.dot(weights[q % 2], spec[q], preferred_element_type=F32).astype(BF16)
        for s in range(count):
            cross[s, q * 2 * GROUP : (q + 1) * 2 * GROUP, :] = product[s * 2 * GROUP : (s + 1) * 2 * GROUP]
    target = lax.broadcasted_iota(jnp.int32, (channels, channels), 0)
    origin = lax.broadcasted_iota(jnp.int32, (channels, channels), 1)
    half = channels // 2
    for s in range(count):
        at = target + offsets[s]
        at = jnp.where(at >= channels, at - channels, at)
        turn = jnp.where(at == origin, 1.0, 0.0).astype(BF16)
        turned = lax.dot_general(
            turn, cross[s], (((1,), (1,)), ((), ())), preferred_element_type=F32
        ).astype(BF16)
        mine[s] = turned[:half]
        other[s] = turned[half:]


STEP = 8


@functools.lru_cache(None)
def factor_table():
    basis = forward_basis()
    real, imag = basis[:, :SEG], basis[:, SEG:]
    order = bin_order()
    straight = basis[:, order].reshape(SEG, -1, STEP * 2 * GROUP)
    crossed = np.concatenate([-imag, real], axis=1)[:, order].reshape(SEG, -1, STEP * 2 * GROUP)
    return np.ascontiguousarray(np.concatenate([straight, crossed], axis=2).transpose(1, 0, 2))


def cross_terms(offsets, blocks, sources, first, steps):
    seg_count, _, channels = blocks.shape
    count = offsets.shape[0]
    width = STEP * 2 * GROUP
    depth = seg_count * 2 * GROUP
    rows = forward_basis().T[bin_order()]
    basis = jnp.asarray(np.ascontiguousarray(rows[first * width : (first + steps) * width]))
    factors = jnp.asarray(factor_table()[first : first + steps])
    half = jax.ShapeDtypeStruct((count, channels // 2, steps * width), BF16)
    half_spec = pl.BlockSpec((count, channels // 2, width), lambda i, o: (0, 0, i))
    return pl.pallas_call(
        cross_kernel,
        grid_spec=pltpu.PrefetchScalarGridSpec(
            num_scalar_prefetch=1,
            grid=(steps,),
            in_specs=[
                pl.BlockSpec((width, SEG), lambda i, o: (i, 0)),
                pl.BlockSpec((1, SEG, 2 * width), lambda i, o: (i, 0, 0)),
                pl.BlockSpec((seg_count, SEG, channels), lambda i, o: (0, 0, 0)),
                pl.BlockSpec(sources.shape, lambda i, o: (0, 0)),
            ],
            out_specs=[half_spec, half_spec],
            scratch_shapes=[
                pltpu.VMEM((STEP, depth, channels), BF16),
                pltpu.VMEM((sources.shape[0], 2 * width), F32),
                pltpu.VMEM((2, count * 2 * GROUP, depth), BF16),
                pltpu.VMEM((count, width, channels), BF16),
            ],
        ),
        out_shape=[half, half],
        cost_estimate=pl.CostEstimate(
            flops=steps * 4_500_000_000, bytes_accessed=steps * 4_000_000, transcendentals=0
        ),
        compiler_params=pltpu.CompilerParams(vmem_limit_bytes=48 * 2**20),
    )(offsets, basis, factors, blocks, sources)


def lag_kernel(kept, came, high, low, out):
    total = kept[...].astype(F32) + came[...].astype(F32)
    top = total.astype(BF16)
    rest = (total - top.astype(F32)).astype(BF16)
    result = jnp.dot(top, low[...], preferred_element_type=F32)
    result = result + jnp.dot(rest, high[...], preferred_element_type=F32)
    out[...] = result + jnp.dot(top, high[...], preferred_element_type=F32)


def lag_product(kept, came, high, low):
    rows, depth = kept.shape
    width = 512
    return pl.pallas_call(
        lag_kernel,
        grid=(2 * SEG // width,),
        in_specs=[
            pl.BlockSpec((rows, depth), lambda i: (0, 0)),
            pl.BlockSpec((rows, depth), lambda i: (0, 0)),
            pl.BlockSpec((depth, width), lambda i: (0, i)),
            pl.BlockSpec((depth, width), lambda i: (0, i)),
        ],
        out_specs=pl.BlockSpec((rows, width), lambda i: (0, i)),
        out_shape=jax.ShapeDtypeStruct((rows, 2 * SEG), F32),
        compiler_params=pltpu.CompilerParams(vmem_limit_bytes=48 * 2**20),
    )(kept, came, high, low)


def passed_along(block, axis, distance):
    devices = range(lax.axis_size(axis))
    route = [(i - distance, i) for i in devices if i - distance in devices]
    return lax.ppermute(block, axis, route)


def swapped(block, bit):
    return lax.ppermute(block, "win", [(i, i ^ bit) for i in range(lax.axis_size("win"))])


def source_rows(samples, exponents, alive, offsets):
    picked = [
        [lax.dynamic_slice_in_dim(a, offsets[j], 1, 0) for j in range(offsets.shape[0])]
        for a in (samples, exponents, alive)
    ]
    samples, exponents, alive = (jnp.concatenate(p, axis=0) for p in picked)
    count, windows, length = samples.shape
    scale = jnp.left_shift(1, exponents).astype(F32)
    amplitude = samples.astype(F32).reshape(count, windows, -1, SCALE_LEN) * scale[..., None]
    energy = jnp.mean(amplitude * amplitude, axis=(2, 3), keepdims=True)
    factor = alive.astype(F32)[:, None, None, None] * lax.rsqrt(energy + 1e-06)
    normed = (amplitude * factor).astype(BF16).reshape(count, windows * length)
    tail = jnp.broadcast_to(offsets.astype(BF16)[:, None], (count, 128))
    return jnp.concatenate([normed, tail], axis=1)


def chan_first(pair, low_part, side, here):
    below = passed_along(pair[2 * here :], "chan", 1)
    above = passed_along(pair[:here], "chan", -1)
    yield below, above
    below, above = yield
    own = pair[here : 2 * here]
    first = jnp.where(low_part, below, own)
    second = jnp.where(low_part, own, above)
    kept = jnp.where(side == 0, first, second)
    yield kept, swapped(jnp.where(side == 0, second, first), 2)


def side_first(pair, low_part, side, here):
    lower, upper = pair[: 2 * here], pair[here:]
    came = swapped(jnp.where(side == 0, lower, upper), 2)
    yield (came,)
    (came,) = yield
    own = pair[here : 2 * here]
    outer = jnp.where(side == 0, pair[2 * here :], pair[:here])
    came_own = jnp.where(side == 0, came[:here], came[here:])
    came_outer = jnp.where(side == 0, came[here:], came[:here])
    outer = (outer.astype(F32) + came_outer.astype(F32)).astype(BF16)
    chans, wins = lax.axis_size("chan"), lax.axis_size("win")
    route = [
        (d * wins + w, e * wins + w)
        for d in range(chans)
        for w in range(wins)
        for e in [d + 1 if w // 2 == 0 else d - 1]
        if 0 <= e < chans
    ]
    came_over = lax.ppermute(outer, ("chan", "win"), route)
    over = low_part == (side == 0)
    yield jnp.where(over, came_over, own), jnp.where(over, jnp.zeros_like(own), came_own)


PLAN = (chan_first, side_first, chan_first, side_first)


def shards(samples, exponents, alive, offsets):
    channels, windows, length = samples.shape
    here = offsets.shape[0]
    win = lax.axis_index("win")
    core, side = win % 2, win // 2
    half = channels // 2
    seg_count = windows * length // SEG
    own = source_rows(samples, exponents, alive, offsets)
    sources = jnp.concatenate(
        [passed_along(own, "chan", 1), own, passed_along(own, "chan", -1)], axis=0
    )
    places = sources[:, windows * length].astype(jnp.int32) + core * half
    places = jnp.where(places >= channels, places - channels, places)
    count = places.shape[0]
    sources = jnp.swapaxes(sources[:, : windows * length].reshape(count, seg_count, SEG), 0, 1)
    sources = jnp.pad(sources, ((0, 0), (0, -count % 16), (0, 0))).reshape(-1, SEG)
    blocks = normalize_blocks(samples, exponents, alive)
    turned = (core * half + jnp.arange(half, dtype=jnp.int32))[None, :, None]
    low_part = turned < (channels - offsets)[:, None, None]
    kept, came = [], []
    steps = SEG // GROUP // STEP // len(PLAN)
    pairs, ways, hops = [], [], []
    for c in range(len(PLAN)):
        if c >= 2:
            places, pairs[c - 2] = lax.optimization_barrier((places, pairs[c - 2]))
            ways.append(PLAN[c - 2](pairs[c - 2], low_part, side, here))
            hops.append(next(ways[-1]))
        if c >= 3:
            places, hops[c - 3] = lax.optimization_barrier((places, hops[c - 3]))
        mine, other = cross_terms(places, blocks, sources, c * steps, steps)
        places, other = lax.optimization_barrier((places, other))
        pairs.append((mine.astype(F32) + swapped(other, 1).astype(F32)).astype(BF16))
    for c in range(len(PLAN)):
        if c >= len(ways):
            ways.append(PLAN[c](pairs[c], low_part, side, here))
            hops.append(next(ways[-1]))
        next(ways[c])
        a, b = ways[c].send(hops[c])
        kept.append(a)
        came.append(b)
    kept = jnp.concatenate(kept, axis=-1).reshape(here * half, 2 * SEG)
    came = jnp.concatenate(came, axis=-1).reshape(here * half, 2 * SEG)
    high, low = lag_tables(windows * lax.axis_size("win"), length // SEG)
    result = lag_product(kept, came, jnp.asarray(high), jnp.asarray(low))
    return result.reshape(here, half, 2 * SEG)


def solution(mesh):
    placed = (P("chan", "win", None), P("chan", "win", None), P("chan"), P("chan"))
    return jax.shard_map(
        shards, mesh=mesh, in_specs=placed, out_specs=P("chan", "win", None), check_vma=False
    )
```
